32 devices in a mesh: wide: 4 (over z), narrow: 8 (over y, x, core).
Axes of the slice: x: 2, y: 2, z: 4, core: 2. Of those that a mesh axis runs over, the one named last changes fastest.
Arguments:
- tokens: bfloat16 [4096, 8192], P(('wide', 'narrow')), may hold values from -24 to 24, as said below
- row_cells: int32 [4096], replicated, may hold values from 0 to 4095, as said below
- documents: int32 [4096], replicated, may hold values from 0 to 3, never falling along the last dimension, each value on 1 to 3072 neighbouring positions
- query_weight: bfloat16 [8192, 512], replicated, as said below
- key_weight: bfloat16 [8192, 128], replicated, as said below
- value_weight: bfloat16 [8192, 128], replicated, may hold values from -0.0625 to 0.0625
Outputs:
- mixed: bfloat16 [4096, 512], P(('wide', 'narrow'))
The draws below stay inside these ranges and needn't reach their ends.
Inputs may be any that keep to these rules, and one draw needn't show every extreme that they name: `row_cells`: a permutation of the cells; the rows of one device go to every device's 128 cells in equal numbers, 4 rows to each, where cells 128 * d to 128 * d + 127 are device d's. `tokens`: activations. `query_weight`: scaled by the width. `key_weight`: scaled by the width.
All inputs are finite; a program needn't handle non-finite values.
Results may differ from the reference program's by a relative error of at most 0.0063.
Values may be sent and summed in bfloat16 or wider, within the bound.
A program may use at most 128 MiB of HBM per device.

```python
import math
import jax
import jax.numpy as jnp
import numpy as np
from jax import lax

D = 8192
HD = 128
QH = 4
TOK_DEV = 128
TOKENS = 4096
DOCS = 4
DOC_MOST = 3072


def common_block(key):
    return jax.random.normal(jax.random.fold_in(key, 101), (D, HD), jnp.float32) * D ** (-0.5)


def draw_key_weight(key, part):
    shared = common_block(key)
    return shared.astype(jnp.bfloat16)


def draw_query_weight(key, part):
    key = jax.random.fold_in(key, 3)
    separate = jax.random.normal(key, (D, QH, HD), jnp.float32) * D ** (-0.5)
    mixture = separate
    return mixture.reshape(D, QH * HD).astype(jnp.bfloat16)


def draw_tokens(key, part):
    key = jax.random.fold_in(key, 5)
    first = jax.random.fold_in(key, 0)
    rows = jnp.clip(jax.random.normal(first, (TOKENS, D), jnp.float32), -6.0, 6.0)
    return rows.astype(jnp.bfloat16)


def draw_row_cells(key, part):
    key = jax.random.fold_in(key, 7)
    devices = TOKENS // TOK_DEV
    per_pair = TOK_DEV // devices
    first, second = jax.random.split(key)
    sender_order = jax.vmap(lambda single: jax.random.permutation(single, TOK_DEV))(jax.random.split(first, devices))
    target = sender_order % devices
    ranking = sender_order // devices
    source = jnp.arange(devices, dtype=jnp.int32)[:, None]
    slot_before = source * per_pair + ranking
    shuffle = jax.vmap(lambda single: jax.random.permutation(single, TOK_DEV))(jax.random.split(second, devices))
    slot = shuffle[target, slot_before]
    return (target * TOK_DEV + slot).reshape(TOKENS).astype(jnp.int32)


def split_up(count, total, most, slope):
    loads = [(1 << 20) // math.isqrt(rank ** slope) + 1 for rank in range(2, count + 1)]
    spare, counts = total - most - (count - 1), [1] * (count - 1)
    while spare > 0:
        free = [i for i in range(count - 1) if counts[i] < most]
        whole, left = sum([loads[i] for i in free]), spare
        for i in free:
            extra = min(most - counts[i], max(1, left * loads[i] // whole), spare)
            counts[i] = counts[i] + extra
            spare = spare - extra
    return np.array([most] + counts)


def ragged(stream_key, count, total, most, lean):
    if count == 2:
        one = jax.random.randint(stream_key, (), max(1, total - most), min(most, total - 1) + 1)
        return jnp.stack([one, total - one])
    tallies = jnp.asarray(split_up(count, total, most, lean), jnp.int32)
    pairs = (count - 1) // 2
    giver, sink = tallies[1:1 + 2 * pairs:2], tallies[2:2 + 2 * pairs:2]
    room = jnp.minimum(giver - 1, most - sink)
    shifted = jax.random.randint(jax.random.fold_in(stream_key, 1), (pairs,), 0, 1 << 20) % (room + 1)
    tallies = tallies.at[1:1 + 2 * pairs:2].set(giver - shifted).at[2:2 + 2 * pairs:2].set(sink + shifted)
    return tallies[jax.random.permutation(jax.random.fold_in(stream_key, 2), count)]


def bell_draw(rng, extent, spread, most, kind=jnp.bfloat16):
    array = spread * jax.random.normal(rng, extent, jnp.float32)
    return jnp.clip(array, min=-most, max=most).astype(kind)


def setup_inputs(seed: int = 0) -> dict:
    seeds = jax.random.split(jax.random.key(seed), 7)
    return {
        "tokens": draw_tokens(jax.random.fold_in(seeds[6], 71), 0),
        "row_cells": draw_row_cells(jax.random.fold_in(seeds[6], 71), 0),
        "documents": jnp.searchsorted(jnp.cumsum(ragged(seeds[2], DOCS, TOKENS, DOC_MOST, 2)), jnp.arange(TOKENS), side="right").astype(jnp.int32),
        "query_weight": draw_query_weight(jax.random.fold_in(seeds[6], 71), 0),
        "key_weight": draw_key_weight(jax.random.fold_in(seeds[6], 71), 0),
        "value_weight": bell_draw(seeds[5], (D, HD), D ** -0.5, 0.0625),
    }


neg_large = -1.0e30


def reference(tokens, row_cells, documents, query_weight, key_weight, value_weight):
    packed = jnp.zeros_like(tokens).at[row_cells].set(tokens)

    def project(weight):
        return jnp.dot(packed, weight, preferred_element_type=jnp.float32).astype(jnp.bfloat16)

    query = project(query_weight).astype(jnp.float32).reshape(TOKENS, QH, HD)
    keys = project(key_weight).astype(jnp.float32)
    values = project(value_weight).astype(jnp.float32)
    block_rows = min(256, TOKENS)
    window = min(DOC_MOST + block_rows, TOKENS)
    score_scale = HD ** -0.5

    def one_block(block):
        first_row = (block * block_rows).astype(jnp.int32)
        key_first = jnp.clip(first_row + block_rows - window, 0, TOKENS - window).astype(jnp.int32)
        block_query = lax.dynamic_slice_in_dim(query, first_row, block_rows, 0)
        block_keys = lax.dynamic_slice_in_dim(keys, key_first, window, 0)
        block_values = lax.dynamic_slice_in_dim(values, key_first, window, 0)
        query_pos = first_row + jnp.arange(block_rows, dtype=jnp.int32)
        key_pos = key_first + jnp.arange(window, dtype=jnp.int32)
        query_docs = lax.dynamic_slice_in_dim(documents, first_row, block_rows, 0)
        key_docs = lax.dynamic_slice_in_dim(documents, key_first, window, 0)
        scores = jnp.einsum("qhd,kd->qhk", block_query, block_keys) * score_scale
        visible = (key_pos[None, :] <= query_pos[:, None]) & (key_docs[None, :] == query_docs[:, None])
        scores = jnp.where(visible[:, None, :], scores, neg_large)
        highest = jnp.max(scores, axis=2, keepdims=True)
        expo = jnp.where(visible[:, None, :], jnp.exp(scores - highest), 0.0)
        total = jnp.sum(expo, axis=2)
        weights = lax.optimization_barrier(expo.astype(jnp.bfloat16)).astype(jnp.float32)
        summed = jnp.einsum("qhk,kd->qhd", weights, block_values)
        return (summed / total[:, :, None]).reshape(block_rows, QH * HD).astype(jnp.bfloat16)

    mixed = lax.map(one_block, jnp.arange(TOKENS // block_rows, dtype=jnp.int32))
    return mixed.reshape(TOKENS, QH * HD)
```

```python
import functools
import jax
import jax.numpy as jnp
from jax import lax
from jax.experimental import pallas as pl
from jax.experimental.pallas import tpu as pltpu
from jax.sharding import PartitionSpec as P

MESH = pl.DeviceIdType.MESH
LOG2E = 1.4426950408889634
HIDDEN = -3e38
LOWEST = -1e38
CHUNKS = 8


def column_of(row, size):
    diag = lax.broadcasted_iota(jnp.int32, (size, size), 0) == lax.broadcasted_iota(
        jnp.int32, (size, size), 1
    )
    return jnp.sum(jnp.where(diag, row, 0), axis=1, keepdims=True)


def row_of(column, size):
    diag = lax.broadcasted_iota(jnp.int32, (size, size), 0) == lax.broadcasted_iota(
        jnp.int32, (size, size), 1
    )
    return jnp.sum(jnp.where(diag, column, 0), axis=0, keepdims=True)


def kernel(
    dims,
    tokens_ref, cells_ref, docs_ref, wq_ref, wk_ref, wv_ref, out_ref,
    tok, wkv, wq, kv, qsend, qrecv, query, maxima, totals, sums,
    local_sem, kv_recv, kv_send, q_send, q_recv,
):
    wide, narrow, rows, heads, size, block = dims
    devices = wide * narrow
    pair = rows // devices
    outer = narrow // 4
    depth = tok.shape[2]
    w = lax.axis_index("wide")
    p = lax.axis_index("narrow")
    me = w * narrow + p
    core = lax.rem(p, 2)
    b = lax.rem(p // 2, 2)
    a = p // 4
    flip_core = 1 - 2 * core
    flip_b = 2 - 4 * b

    def firsts(q, c):
        if outer == 2:
            qa, qb = q // 4, lax.rem(q // 2, 2)
            return q + (2 - 4 * qb) * (1 - c) + (4 - 8 * qa) * c
        return q + 2 - 4 * lax.rem(q // 2, 2)

    def second_list(q, c):
        if outer == 2:
            qa, qb = q // 4, lax.rem(q // 2, 2)
            return [q + (4 - 8 * qa) * (1 - c) + (2 - 4 * qb) * c]
        return [lax.rem(q + 4 * step, narrow) for step in range(1, outer)]

    sibling = p + flip_core
    first = firsts(p, core)
    seconds = second_list(p, core)

    barrier = pltpu.get_barrier_semaphore()

    def greet(step, carry):
        other = lax.rem(me + step, devices)
        pl.semaphore_signal(
            barrier, inc=1, device_id=(other // narrow, lax.rem(other, narrow)), device_id_type=MESH
        )
        return carry

    def chunk_copies(c):
        span = pl.ds(c * depth, depth)
        return [
            pltpu.make_async_copy(tokens_ref.at[:, span], tok.at[c], local_sem.at[0, c]),
            pltpu.make_async_copy(wk_ref.at[span, :], wkv.at[c, :, pl.ds(0, size)], local_sem.at[1, c]),
            pltpu.make_async_copy(wv_ref.at[span, :], wkv.at[c, :, pl.ds(size, size)], local_sem.at[2, c]),
        ]

    def query_copy(c):
        span = pl.ds(c * depth, depth)
        return pltpu.make_async_copy(wq_ref.at[span, :], wq.at[c], local_sem.at[3, c])

    for c in range(CHUNKS):
        for copy in chunk_copies(c):
            copy.start()
    for c in range(CHUNKS):
        query_copy(c).start()
    lax.fori_loop(1, devices, greet, 0)

    acc = jnp.zeros((rows, 2 * size), jnp.float32)
    for c in range(CHUNKS):
        for copy in chunk_copies(c):
            copy.wait()
        acc = acc + jnp.dot(tok[c], wkv[c], preferred_element_type=jnp.float32)
    kv[p, w] = acc.astype(jnp.bfloat16)

    pl.semaphore_wait(barrier, devices - 1)

    def send(q, u, to_wide, to_narrow, kind):
        pltpu.make_async_remote_copy(
            src_ref=kv.at[q, u],
            dst_ref=kv.at[q, u],
            send_sem=kv_send.at[kind],
            recv_sem=kv_recv.at[q, u],
            device_id=(to_wide, to_narrow),
            device_id_type=MESH,
        ).start()

    def arrived(q, u):
        pltpu.make_async_copy(kv.at[q, u], kv.at[q, u], kv_recv.at[q, u]).wait()

    steps = list(range(1, wide))
    steps.sort(key=lambda step: min(step, wide - step))
    send(p, w, w, first, 1)
    for other in seconds:
        send(p, w, w, other, 2)
    for step in steps:
        send(p, w, lax.rem(w + step, wide), p, 0)
    send(p, w, w, sibling, 3)

    def forward_column():
        for step in steps:
            u = lax.rem(w + wide - step, wide)
            arrived(p, u)
            send(p, u, w, first, 1)
            for other in seconds:
                send(p, u, w, other, 2)
            send(p, u, w, sibling, 3)

    def ordered():
        return [w] + [lax.rem(w + wide - step, wide) for step in steps]

    def forward_first():
        for u in ordered():
            arrived(first, u)
            for other in seconds:
                send(first, u, w, other, 2)
            send(first, u, w, sibling, 3)

    def forward_second(group):
        for u in ordered():
            arrived(group, u)
            send(group, u, w, sibling, 3)

    def take(group):
        for u in ordered():
            arrived(group, u)

    acc_q = jnp.zeros((rows, heads * size), jnp.float32)
    for c in range(CHUNKS):
        query_copy(c).wait()
        acc_q = acc_q + jnp.dot(tok[c], wq[c], preferred_element_type=jnp.float32)
    own_q = acc_q.astype(jnp.bfloat16)
    stacked = jnp.concatenate([own_q[:, h * size:(h + 1) * size] for h in range(heads)], axis=0)

    my_cells = cells_ref[pl.ds(me, 1), :]
    rank = jnp.sum((column_of(my_cells, rows) < my_cells).astype(jnp.int32), axis=0, keepdims=True)
    base_place = rank // pair * block + rank % pair
    place = jnp.concatenate([base_place + h * pair for h in range(heads)], axis=1)
    chosen = lax.broadcasted_iota(jnp.int32, (devices * block, heads * rows), 0) == place
    sorted_q = jnp.dot(
        jnp.where(chosen, 1.0, 0.0).astype(jnp.bfloat16), stacked, preferred_element_type=jnp.float32
    ).astype(jnp.bfloat16)
    qsend[...] = sorted_q.reshape(devices, block, size)

    def give(step, carry):
        other = lax.rem(me + step, devices)
        pltpu.make_async_remote_copy(
            src_ref=qsend.at[other],
            dst_ref=qrecv.at[me],
            send_sem=q_send,
            recv_sem=q_recv,
            device_id=(other // narrow, lax.rem(other, narrow)),
            device_id_type=MESH,
        ).start()
        return carry

    lax.fori_loop(1, devices, give, 0)
    qrecv[me] = qsend[me]

    forward_column()

    base = me * rows
    my_pos = base + lax.broadcasted_iota(jnp.int32, (rows, 1), 0)
    my_docs = column_of(docs_ref[pl.ds(me, 1), :], rows)

    def look(s, carry):
        before, source = carry
        before = before + (docs_ref[pl.ds(s, 1), :] < my_docs).astype(jnp.int32)
        source = source + jnp.where(cells_ref[pl.ds(s, 1), :] == my_pos, s, 0)
        return before, source

    zeros = jnp.zeros((rows, rows), jnp.int32)
    before, source = lax.fori_loop(0, devices, look, (zeros, zeros), unroll=4)
    start = jnp.sum(before, axis=1, keepdims=True)
    source = jnp.sum(source, axis=1, keepdims=True)
    earlier = (row_of(source, rows) == source) & (
        lax.broadcasted_iota(jnp.int32, (rows, rows), 1)
        < lax.broadcasted_iota(jnp.int32, (rows, rows), 0)
    )
    nth = jnp.sum(earlier.astype(jnp.int32), axis=1, keepdims=True)
    lies = source * block + nth
    lies = jnp.concatenate([lies + h * pair for h in range(heads)], axis=0)
    picked = lax.broadcasted_iota(jnp.int32, (heads * rows, devices * block), 1) == lies
    picked = jnp.where(picked, 1.0, 0.0).astype(jnp.bfloat16)

    forward_first()

    pltpu.make_async_copy(
        qrecv.at[pl.ds(0, devices - 1)], qrecv.at[pl.ds(0, devices - 1)], q_recv
    ).wait()
    query[...] = jnp.dot(
        picked, qrecv[...].reshape(devices * block, size), preferred_element_type=jnp.float32
    ).astype(jnp.bfloat16)
    maxima[...] = jnp.full(maxima.shape, LOWEST, jnp.float32)
    totals[...] = jnp.zeros(totals.shape, jnp.float32)
    sums[...] = jnp.zeros(sums.shape, jnp.float32)
    factor = size ** (-0.5) * LOG2E

    def attend(group):
        keys = kv[group, :, :, pl.ds(0, size)].reshape(wide * rows, size)
        values = kv[group, :, :, pl.ds(size, size)].reshape(wide * rows, size)
        cells = jnp.concatenate(
            [cells_ref[pl.ds(u * narrow + group, 1), :] for u in range(wide)], axis=1
        )
        seen = (cells >= start) & (cells <= my_pos)
        for h in range(heads):
            part = pl.ds(h * rows, rows)
            scores = lax.dot_general(
                query[part, :], keys, (((1,), (1,)), ((), ())), preferred_element_type=jnp.float32
            ) * factor
            scores = jnp.where(seen, scores, HIDDEN)
            old = maxima[part, :]
            top = jnp.maximum(old, jnp.max(scores, axis=1, keepdims=True))
            expo = jnp.exp2(scores - top)
            shrink = jnp.exp2(old - top)
            totals[part, :] = totals[part, :] * shrink + jnp.sum(expo, axis=1, keepdims=True)
            sums[part, :] = sums[part, :] * shrink + jnp.dot(
                expo.astype(jnp.bfloat16), values, preferred_element_type=jnp.float32
            )
            maxima[part, :] = top

    attend(p)
    for other in seconds:
        forward_second(other)
    attend(first)
    take(sibling)
    attend(sibling)
    for other in seconds:
        forward_second(firsts(other, core))
    sibling_first = firsts(sibling, 1 - core)
    take(sibling_first)
    attend(sibling_first)
    sibling_seconds = second_list(sibling, 1 - core)
    for other in seconds:
        attend(other)
    for other in sibling_seconds:
        take(other)
        attend(other)
    for other in seconds:
        attend(firsts(other, core))
    for other in sibling_seconds:
        far = firsts(other, 1 - core)
        take(far)
        attend(far)

    for h in range(heads):
        part = pl.ds(h * rows, rows)
        out_ref[:, h * size:(h + 1) * size] = (sums[part, :] / totals[part, :]).astype(jnp.bfloat16)

    spans = (kv.at[0, pl.ds(0, wide - 1)], kv.at[0], kv.at[pl.ds(0, 2 * (outer - 1))], kv.at[pl.ds(0, narrow // 2)])
    for kind, span in enumerate(spans):
        pltpu.make_async_copy(span, span, kv_send.at[kind]).wait()
    pltpu.make_async_copy(
        qsend.at[pl.ds(0, devices - 1)], qsend.at[pl.ds(0, devices - 1)], q_send
    ).wait()


def solution(mesh):
    wide, narrow = mesh.shape["wide"], mesh.shape["narrow"]
    devices = wide * narrow

    def shards(tokens, row_cells, documents, query_weight, key_weight, value_weight):
        rows, width = tokens.shape
        size = key_weight.shape[1]
        heads = query_weight.shape[1] // size
        pair = rows // devices
        block = -(-pair * heads // 16) * 16
        depth = width // CHUNKS
        dims = (wide, narrow, rows, heads, size, block)
        vmem = pl.BlockSpec(memory_space=pltpu.VMEM)
        hbm = pl.BlockSpec(memory_space=pl.ANY)
        flops = 2 * rows * width * (heads + 2) * size + 4 * rows * heads * devices * rows * size
        return pl.pallas_call(
            functools.partial(kernel, dims),
            out_shape=jax.ShapeDtypeStruct((rows, heads * size), jnp.bfloat16),
            in_specs=[hbm, vmem, vmem, hbm, hbm, hbm],
            out_specs=vmem,
            scratch_shapes=[
                pltpu.VMEM((CHUNKS, rows, depth), jnp.bfloat16),
                pltpu.VMEM((CHUNKS, depth, 2 * size), jnp.bfloat16),
                pltpu.VMEM((CHUNKS, depth, heads * size), jnp.bfloat16),
                pltpu.VMEM((narrow, wide, rows, 2 * size), jnp.bfloat16),
                pltpu.VMEM((devices, block, size), jnp.bfloat16),
                pltpu.VMEM((devices, block, size), jnp.bfloat16),
                pltpu.VMEM((heads * rows, size), jnp.bfloat16),
                pltpu.VMEM((heads * rows, 1), jnp.float32),
                pltpu.VMEM((heads * rows, 1), jnp.float32),
                pltpu.VMEM((heads * rows, size), jnp.float32),
                pltpu.SemaphoreType.DMA((4, CHUNKS)),
                pltpu.SemaphoreType.DMA((narrow, wide)),
                pltpu.SemaphoreType.DMA((4,)),
                pltpu.SemaphoreType.DMA,
                pltpu.SemaphoreType.DMA,
            ],
            compiler_params=pltpu.CompilerParams(
                collective_id=0, has_side_effects=True, vmem_limit_bytes=56 * 1024 * 1024
            ),
            cost_estimate=pl.CostEstimate(
                flops=flops, bytes_accessed=16 * 1024 * 1024, transcendentals=rows * heads * devices * rows
            ),
        )(
            tokens,
            row_cells.reshape(devices, rows),
            documents.reshape(devices, rows),
            query_weight,
            key_weight,
            value_weight,
        )

    in_specs = (P(("wide", "narrow"), None), P(), P(), P(), P(), P())
    return jax.shard_map(
        shards, mesh=mesh, in_specs=in_specs, out_specs=P(("wide", "narrow"), None), check_vma=False
    )
```

```python
import functools
import jax
import jax.numpy as jnp
from jax import lax
from jax.experimental import pallas as pl
from jax.experimental.pallas import tpu as pltpu
from jax.sharding import PartitionSpec as P

MESH = pl.DeviceIdType.MESH
LOG2E = 1.4426950408889634
HIDDEN = -3e38
LOWEST = -1e38
CHUNKS = 8


def column_of(row, size):
    diag = lax.broadcasted_iota(jnp.int32, (size, size), 0) == lax.broadcasted_iota(
        jnp.int32, (size, size), 1
    )
    return jnp.sum(jnp.where(diag, row, 0), axis=1, keepdims=True)


def row_of(column, size):
    diag = lax.broadcasted_iota(jnp.int32, (size, size), 0) == lax.broadcasted_iota(
        jnp.int32, (size, size), 1
    )
    return jnp.sum(jnp.where(diag, column, 0), axis=0, keepdims=True)


def kernel(
    dims,
    tokens_ref, cells_ref, docs_ref, wq_ref, wk_ref, wv_ref, out_ref,
    tok, wkv, wq, kv, qsend, qmid, qrecv, query, maxima, sums,
    local_sem, kv_recv, kv_send, q_send, q_recv,
):
    wide, narrow, rows, heads, size, block = dims
    devices = wide * narrow
    pair = rows // devices
    outer = narrow // 4
    depth = tok.shape[2]
    w = lax.axis_index("wide")
    p = lax.axis_index("narrow")
    me = w * narrow + p
    core = lax.rem(p, 2)
    b = lax.rem(p // 2, 2)
    a = p // 4
    flip_core = 1 - 2 * core
    flip_b = 2 - 4 * b

    def firsts(q, c):
        if outer == 2:
            qa, qb = q // 4, lax.rem(q // 2, 2)
            return q + (2 - 4 * qb) * (1 - c) + (4 - 8 * qa) * c
        return q + 2 - 4 * lax.rem(q // 2, 2)

    def second_list(q, c):
        if outer == 2:
            qa, qb = q // 4, lax.rem(q // 2, 2)
            return [q + (4 - 8 * qa) * (1 - c) + (2 - 4 * qb) * c]
        return [lax.rem(q + 4 * step, narrow) for step in range(1, outer)]

    sibling = p + flip_core
    first = firsts(p, core)
    seconds = second_list(p, core)

    barrier = pltpu.get_barrier_semaphore()

    def greet(to_wide, to_narrow):
        pl.semaphore_signal(
            barrier, inc=1, device_id=(to_wide, to_narrow), device_id_type=MESH
        )

    for step in range(1, narrow):
        greet(w, lax.rem(p + step, narrow))
    for step in range(1, wide):
        greet(lax.rem(w + step, wide), p)

    def chunk_copies(c):
        span = pl.ds(c * depth, depth)
        return [
            pltpu.make_async_copy(tokens_ref.at[:, span], tok.at[c], local_sem.at[0, c]),
            pltpu.make_async_copy(wk_ref.at[span, :], wkv.at[c, :, pl.ds(0, size)], local_sem.at[1, c]),
            pltpu.make_async_copy(wv_ref.at[span, :], wkv.at[c, :, pl.ds(size, size)], local_sem.at[2, c]),
        ]

    def query_copy(c):
        span = pl.ds(c * depth, depth)
        return pltpu.make_async_copy(wq_ref.at[span, :], wq.at[c], local_sem.at[3, c])

    for c in range(CHUNKS):
        for copy in chunk_copies(c):
            copy.start()
    for c in range(CHUNKS):
        query_copy(c).start()

    my_cells = cells_ref[pl.ds(me, 1), :]
    rank = jnp.sum((column_of(my_cells, rows) < my_cells).astype(jnp.int32), axis=0, keepdims=True)
    base_place = rank // pair * block + rank % pair
    place = jnp.concatenate([base_place + h * pair for h in range(heads)], axis=1)

    base = me * rows
    my_pos = base + lax.broadcasted_iota(jnp.int32, (rows, 1), 0)
    my_docs = column_of(docs_ref[pl.ds(me, 1), :], rows)

    def look(s, carry):
        before, source = carry
        before = before + (docs_ref[pl.ds(s, 1), :] < my_docs).astype(jnp.int32)
        source = source + jnp.where(cells_ref[pl.ds(s, 1), :] == my_pos, s, 0)
        return before, source

    zeros = jnp.zeros((rows, rows), jnp.int32)
    before, source = lax.fori_loop(0, devices, look, (zeros, zeros), unroll=4)
    start = jnp.sum(before, axis=1, keepdims=True)
    source = jnp.sum(source, axis=1, keepdims=True)
    earlier = (row_of(source, rows) == source) & (
        lax.broadcasted_iota(jnp.int32, (rows, rows), 1)
        < lax.broadcasted_iota(jnp.int32, (rows, rows), 0)
    )
    nth = jnp.sum(earlier.astype(jnp.int32), axis=1, keepdims=True)
    lies = (source % narrow * wide + source // narrow) * block + nth
    lies = jnp.concatenate([lies + h * pair for h in range(heads)], axis=0)

    acc = jnp.zeros((rows, 2 * size), jnp.float32)
    for c in range(CHUNKS):
        for copy in chunk_copies(c):
            copy.wait()
        acc = acc + jnp.dot(tok[c], wkv[c], preferred_element_type=jnp.float32)
    kv[p, w] = acc.astype(jnp.bfloat16)

    pl.semaphore_wait(barrier, narrow + wide - 2)

    def send(q, u, to_wide, to_narrow, kind):
        pltpu.make_async_remote_copy(
            src_ref=kv.at[q, u],
            dst_ref=kv.at[q, u],
            send_sem=kv_send.at[kind],
            recv_sem=kv_recv.at[q, u],
            device_id=(to_wide, to_narrow),
            device_id_type=MESH,
        ).start()

    def arrived(q, u):
        pltpu.make_async_copy(kv.at[q, u], kv.at[q, u], kv_recv.at[q, u]).wait()

    steps = list(range(1, wide))
    steps.sort(key=lambda step: min(step, wide - step))
    send(p, w, w, first, 1)
    for other in seconds:
        send(p, w, w, other, 2)
    for step in steps:
        send(p, w, lax.rem(w + step, wide), p, 0)
    send(p, w, w, sibling, 3)

    sources = [w] + [lax.rem(w + wide - step, wide) for step in steps]

    def pass_column(u):
        arrived(p, u)
        send(p, u, w, first, 1)
        for other in seconds:
            send(p, u, w, other, 2)
        send(p, u, w, sibling, 3)

    def pass_first(u):
        arrived(first, u)
        for other in seconds:
            send(first, u, w, other, 2)
        send(first, u, w, sibling, 3)

    def forward_second(group):
        for u in sources:
            arrived(group, u)
            send(group, u, w, sibling, 3)

    def take(group):
        for u in sources:
            arrived(group, u)

    acc_q = jnp.zeros((rows, heads * size), jnp.float32)
    for c in range(CHUNKS):
        query_copy(c).wait()
        acc_q = acc_q + jnp.dot(tok[c], wq[c], preferred_element_type=jnp.float32)
        if c == CHUNKS // 2:
            for u in sources[1:3]:
                pass_column(u)
            pass_first(w)
    own_q = acc_q.astype(jnp.bfloat16)
    stacked = jnp.concatenate([own_q[:, h * size:(h + 1) * size] for h in range(heads)], axis=0)

    chosen = lax.broadcasted_iota(jnp.int32, (devices * block, heads * rows), 0) == place
    sorted_q = jnp.dot(
        jnp.where(chosen, 1.0, 0.0).astype(jnp.bfloat16), stacked, preferred_element_type=jnp.float32
    ).astype(jnp.bfloat16)
    qsend[...] = sorted_q.reshape(wide, narrow, block, size)
    for step in steps:
        other = lax.rem(w + step, wide)
        pltpu.make_async_remote_copy(
            src_ref=qsend.at[other],
            dst_ref=qmid.at[w],
            send_sem=q_send.at[0],
            recv_sem=q_recv.at[0],
            device_id=(other, p),
            device_id_type=MESH,
        ).start()
    qmid[w] = qsend[w]

    for u in sources[3:]:
        pass_column(u)
    for u in sources[1:3]:
        pass_first(u)

    waited = qmid.at[pl.ds(0, wide - 1)]
    pltpu.make_async_copy(waited, waited, q_recv.at[0]).wait()
    for step in range(1, narrow):
        other = lax.rem(p + step, narrow)
        pltpu.make_async_remote_copy(
            src_ref=qmid.at[:, other],
            dst_ref=qrecv.at[p],
            send_sem=q_send.at[1],
            recv_sem=q_recv.at[1],
            device_id=(w, other),
            device_id_type=MESH,
        ).start()
    qrecv[p] = qmid[:, pl.ds(p, 1)].reshape(wide, block, size)
    for u in sources[3:]:
        pass_first(u)

    picked = lax.broadcasted_iota(jnp.int32, (heads * rows, devices * block), 1) == lies
    picked = jnp.where(picked, 1.0, 0.0).astype(jnp.bfloat16)

    waited = qrecv.at[pl.ds(0, narrow - 1)]
    pltpu.make_async_copy(waited, waited, q_recv.at[1]).wait()
    query[...] = jnp.dot(
        picked, qrecv[...].reshape(devices * block, size), preferred_element_type=jnp.float32
    ).astype(jnp.bfloat16)
    maxima[...] = jnp.full(maxima.shape, LOWEST, jnp.float32)
    sums[...] = jnp.zeros(sums.shape, jnp.float32)
    factor = size ** (-0.5) * LOG2E

    def attend(group):
        keys = kv[group, :, :, pl.ds(0, size)].reshape(wide * rows, size)
        values = kv[group, :, :, pl.ds(size, size)].reshape(wide * rows, size)
        cells = jnp.concatenate(
            [cells_ref[pl.ds(u * narrow + group, 1), :] for u in range(wide)], axis=1
        )
        seen = (cells >= start) & (cells <= my_pos)
        wider = jnp.concatenate([values, jnp.ones_like(values)], axis=1)
        scores = lax.dot_general(
            query[...], keys, (((1,), (1,)), ((), ())), preferred_element_type=jnp.float32
        )
        expos, shrinks = [], []
        for h in range(heads):
            part = pl.ds(h * rows, rows)
            shown = jnp.where(seen, scores[h * rows:(h + 1) * rows] * factor, HIDDEN)
            old = maxima[part, :]
            top = jnp.maximum(old, jnp.max(shown, axis=1, keepdims=True))
            expos.append(jnp.exp2(shown - top).astype(jnp.bfloat16))
            shrinks.append(jnp.exp2(old - top))
            maxima[part, :] = top
        product = jnp.dot(
            jnp.concatenate(expos, axis=0), wider, preferred_element_type=jnp.float32
        )
        for h in range(heads):
            part = pl.ds(h * rows, rows)
            sums[part, :] = sums[part, :] * shrinks[h] + product[h * rows:(h + 1) * rows]

    attend(p)
    for other in seconds:
        forward_second(other)
    attend(first)
    take(sibling)
    attend(sibling)
    for other in seconds:
        forward_second(firsts(other, core))
    sibling_first = firsts(sibling, 1 - core)
    take(sibling_first)
    attend(sibling_first)
    sibling_seconds = second_list(sibling, 1 - core)
    for other in seconds:
        attend(other)
    for other in sibling_seconds:
        take(other)
        attend(other)
    for other in seconds:
        attend(firsts(other, core))
    for other in sibling_seconds:
        far = firsts(other, 1 - core)
        take(far)
        attend(far)

    for h in range(heads):
        part = pl.ds(h * rows, rows)
        out_ref[:, h * size:(h + 1) * size] = (
            sums[part, pl.ds(0, size)] / sums[part, pl.ds(size, size)]
        ).astype(jnp.bfloat16)

    spans = (kv.at[0, pl.ds(0, wide - 1)], kv.at[0], kv.at[pl.ds(0, 2 * (outer - 1))], kv.at[pl.ds(0, narrow // 2)])
    for kind, span in enumerate(spans):
        pltpu.make_async_copy(span, span, kv_send.at[kind]).wait()
    for kind, span in enumerate((qsend.at[pl.ds(0, wide - 1)], qrecv.at[pl.ds(0, narrow - 1)])):
        pltpu.make_async_copy(span, span, q_send.at[kind]).wait()


def solution(mesh):
    wide, narrow = mesh.shape["wide"], mesh.shape["narrow"]
    devices = wide * narrow

    def shards(tokens, row_cells, documents, query_weight, key_weight, value_weight):
        rows, width = tokens.shape
        size = key_weight.shape[1]
        heads = query_weight.shape[1] // size
        pair = rows // devices
        block = -(-pair * heads // 16) * 16
        depth = width // CHUNKS
        dims = (wide, narrow, rows, heads, size, block)
        vmem = pl.BlockSpec(memory_space=pltpu.VMEM)
        hbm = pl.BlockSpec(memory_space=pl.ANY)
        flops = 2 * rows * width * (heads + 2) * size + 4 * rows * heads * devices * rows * size
        return pl.pallas_call(
            functools.partial(kernel, dims),
            out_shape=jax.ShapeDtypeStruct((rows, heads * size), jnp.bfloat16),
            in_specs=[hbm, vmem, vmem, hbm, hbm, hbm],
            out_specs=vmem,
            scratch_shapes=[
                pltpu.VMEM((CHUNKS, rows, depth), jnp.bfloat16),
                pltpu.VMEM((CHUNKS, depth, 2 * size), jnp.bfloat16),
                pltpu.VMEM((CHUNKS, depth, heads * size), jnp.bfloat16),
                pltpu.VMEM((narrow, wide, rows, 2 * size), jnp.bfloat16),
                pltpu.VMEM((wide, narrow, block, size), jnp.bfloat16),
                pltpu.VMEM((wide, narrow, block, size), jnp.bfloat16),
                pltpu.VMEM((narrow, wide, block, size), jnp.bfloat16),
                pltpu.VMEM((heads * rows, size), jnp.bfloat16),
                pltpu.VMEM((heads * rows, 1), jnp.float32),
                pltpu.VMEM((heads * rows, 2 * size), jnp.float32),
                pltpu.SemaphoreType.DMA((4, CHUNKS)),
                pltpu.SemaphoreType.DMA((narrow, wide)),
                pltpu.SemaphoreType.DMA((4,)),
                pltpu.SemaphoreType.DMA((2,)),
                pltpu.SemaphoreType.DMA((2,)),
            ],
            compiler_params=pltpu.CompilerParams(
                collective_id=0, has_side_effects=True, vmem_limit_bytes=56 * 1024 * 1024
            ),
            cost_estimate=pl.CostEstimate(
                flops=flops, bytes_accessed=16 * 1024 * 1024, transcendentals=rows * heads * devices * rows
            ),
        )(
            tokens,
            row_cells.reshape(devices, rows),
            documents.reshape(devices, rows),
            query_weight,
            key_weight,
            value_weight,
        )

    in_specs = (P(("wide", "narrow"), None), P(), P(), P(), P(), P())
    return jax.shard_map(
        shards, mesh=mesh, in_specs=in_specs, out_specs=P(("wide", "narrow"), None), check_vma=False
    )
```

```python
import functools
import jax
import jax.numpy as jnp
from jax import lax
from jax.experimental import pallas as pl
from jax.experimental.pallas import tpu as pltpu
from jax.sharding import PartitionSpec as P

MESH = pl.DeviceIdType.MESH
LOG2E = 1.4426950408889634
HIDDEN = -3e38
LOWEST = -1e38
CHUNKS = 8


def column_of(row, size):
    diag = lax.broadcasted_iota(jnp.int32, (size, size), 0) == lax.broadcasted_iota(
        jnp.int32, (size, size), 1
    )
    return jnp.sum(jnp.where(diag, row, 0), axis=1, keepdims=True)


def row_of(column, size):
    diag = lax.broadcasted_iota(jnp.int32, (size, size), 0) == lax.broadcasted_iota(
        jnp.int32, (size, size), 1
    )
    return jnp.sum(jnp.where(diag, column, 0), axis=0, keepdims=True)


def kernel(
    dims,
    tokens_ref, cells_ref, docs_ref, wq_ref, wk_ref, wv_ref, out_ref,
    tok, wkv, wq, kv, qsend, qmid, qrecv, query, maxima, sums,
    local_sem, kv_recv, kv_send, q_send, q_recv,
):
    wide, narrow, rows, heads, size, block = dims
    devices = wide * narrow
    pair = rows // devices
    outer = narrow // 4
    depth = tok.shape[2]
    w = lax.axis_index("wide")
    p = lax.axis_index("narrow")
    me = w * narrow + p
    core = lax.rem(p, 2)
    b = lax.rem(p // 2, 2)
    a = p // 4
    flip_core = 1 - 2 * core
    flip_b = 2 - 4 * b

    def firsts(q, c):
        if outer == 2:
            qa, qb = q // 4, lax.rem(q // 2, 2)
            return q + (2 - 4 * qb) * (1 - c) + (4 - 8 * qa) * c
        return q + 2 - 4 * lax.rem(q // 2, 2)

    def second_list(q, c):
        if outer == 2:
            qa, qb = q // 4, lax.rem(q // 2, 2)
            return [q + (4 - 8 * qa) * (1 - c) + (2 - 4 * qb) * c]
        return [lax.rem(q + 4 * step, narrow) for step in range(1, outer)]

    sibling = p + flip_core
    first = firsts(p, core)
    seconds = second_list(p, core)

    barrier = pltpu.get_barrier_semaphore()

    def greet(to_wide, to_narrow):
        pl.semaphore_signal(
            barrier, inc=1, device_id=(to_wide, to_narrow), device_id_type=MESH
        )

    for step in range(1, narrow):
        greet(w, lax.rem(p + step, narrow))
    for step in range(1, wide):
        greet(lax.rem(w + step, wide), p)

    def chunk_copies(c):
        span = pl.ds(c * depth, depth)
        return [
            pltpu.make_async_copy(tokens_ref.at[:, span], tok.at[c], local_sem.at[0, c]),
            pltpu.make_async_copy(wk_ref.at[span, :], wkv.at[c, :, pl.ds(0, size)], local_sem.at[1, c]),
            pltpu.make_async_copy(wv_ref.at[span, :], wkv.at[c, :, pl.ds(size, size)], local_sem.at[2, c]),
        ]

    def query_copy(c):
        span = pl.ds(c * depth, depth)
        return pltpu.make_async_copy(wq_ref.at[span, :], wq.at[c], local_sem.at[3, c])

    for c in range(CHUNKS):
        for copy in chunk_copies(c):
            copy.start()
    for c in range(CHUNKS):
        query_copy(c).start()

    my_cells = cells_ref[pl.ds(me, 1), :]
    rank = jnp.sum((column_of(my_cells, rows) < my_cells).astype(jnp.int32), axis=0, keepdims=True)
    base_place = rank // pair * block + rank % pair
    place = jnp.concatenate([base_place + h * pair for h in range(heads)], axis=1)

    base = me * rows
    my_pos = base + lax.broadcasted_iota(jnp.int32, (rows, 1), 0)
    my_docs = column_of(docs_ref[pl.ds(me, 1), :], rows)

    def look(s, carry):
        before, source = carry
        before = before + (docs_ref[pl.ds(s, 1), :] < my_docs).astype(jnp.int32)
        source = source + jnp.where(cells_ref[pl.ds(s, 1), :] == my_pos, s, 0)
        return before, source

    zeros = jnp.zeros((rows, rows), jnp.int32)
    before, source = lax.fori_loop(0, devices, look, (zeros, zeros), unroll=4)
    start = jnp.sum(before, axis=1, keepdims=True)
    source = jnp.sum(source, axis=1, keepdims=True)
    earlier = (row_of(source, rows) == source) & (
        lax.broadcasted_iota(jnp.int32, (rows, rows), 1)
        < lax.broadcasted_iota(jnp.int32, (rows, rows), 0)
    )
    nth = jnp.sum(earlier.astype(jnp.int32), axis=1, keepdims=True)
    lies = (source % narrow * wide + source // narrow) * block + nth
    lies = jnp.concatenate([lies + h * pair for h in range(heads)], axis=0)

    acc = jnp.zeros((rows, 2 * size), jnp.float32)
    for c in range(CHUNKS):
        for copy in chunk_copies(c):
            copy.wait()
        acc = acc + jnp.dot(tok[c], wkv[c], preferred_element_type=jnp.float32)
    kv[p, w] = acc.astype(jnp.bfloat16)

    pl.semaphore_wait(barrier, narrow + wide - 2)

    def send(q, u, to_wide, to_narrow, kind):
        pltpu.make_async_remote_copy(
            src_ref=kv.at[q, u],
            dst_ref=kv.at[q, u],
            send_sem=kv_send.at[kind],
            recv_sem=kv_recv.at[q, u],
            device_id=(to_wide, to_narrow),
            device_id_type=MESH,
        ).start()

    def arrived(q, u):
        pltpu.make_async_copy(kv.at[q, u], kv.at[q, u], kv_recv.at[q, u]).wait()

    steps = list(range(1, wide))
    steps.sort(key=lambda step: min(step, wide - step))
    send(p, w, w, first, 1)
    for other in seconds:
        send(p, w, w, other, 2)
    for step in steps:
        send(p, w, lax.rem(w + step, wide), p, 0)
    send(p, w, w, sibling, 3)

    sources = [w] + [lax.rem(w + wide - step, wide) for step in steps]

    def pass_column(u):
        arrived(p, u)
        send(p, u, w, first, 1)
        for other in seconds:
            send(p, u, w, other, 2)
        send(p, u, w, sibling, 3)

    def pass_first(u):
        arrived(first, u)
        for other in seconds:
            send(first, u, w, other, 2)
        send(first, u, w, sibling, 3)

    def forward_second(group):
        for u in sources:
            arrived(group, u)
            send(group, u, w, sibling, 3)

    def take(group):
        for u in sources:
            arrived(group, u)

    acc_q = jnp.zeros((rows, heads * size), jnp.float32)
    for c in range(CHUNKS):
        query_copy(c).wait()
        acc_q = acc_q + jnp.dot(tok[c], wq[c], preferred_element_type=jnp.float32)
        if c == CHUNKS // 2:
            for u in sources[1:3]:
                pass_column(u)
            pass_first(w)
    own_q = acc_q.astype(jnp.bfloat16)
    stacked = jnp.concatenate([own_q[:, h * size:(h + 1) * size] for h in range(heads)], axis=0)

    chosen = lax.broadcasted_iota(jnp.int32, (devices * block, heads * rows), 0) == place
    sorted_q = jnp.dot(
        jnp.where(chosen, 1.0, 0.0).astype(jnp.bfloat16), stacked, preferred_element_type=jnp.float32
    ).astype(jnp.bfloat16)
    qsend[...] = sorted_q.reshape(wide, narrow, block, size)
    for step in steps:
        other = lax.rem(w + step, wide)
        pltpu.make_async_remote_copy(
            src_ref=qsend.at[other],
            dst_ref=qmid.at[w],
            send_sem=q_send.at[0],
            recv_sem=q_recv.at[0],
            device_id=(other, p),
            device_id_type=MESH,
        ).start()
    qmid[w] = qsend[w]

    for u in sources[3:]:
        pass_column(u)
    for u in sources[1:3]:
        pass_first(u)

    waited = qmid.at[pl.ds(0, wide - 1)]
    pltpu.make_async_copy(waited, waited, q_recv.at[0]).wait()
    for step in range(1, narrow):
        other = lax.rem(p + step, narrow)
        pltpu.make_async_remote_copy(
            src_ref=qmid.at[:, other],
            dst_ref=qrecv.at[p],
            send_sem=q_send.at[1],
            recv_sem=q_recv.at[1],
            device_id=(w, other),
            device_id_type=MESH,
        ).start()
    qrecv[p] = qmid[:, pl.ds(p, 1)].reshape(wide, block, size)
    for u in sources[3:]:
        pass_first(u)

    picked = lax.broadcasted_iota(jnp.int32, (heads * rows, devices * block), 1) == lies
    picked = jnp.where(picked, 1.0, 0.0).astype(jnp.bfloat16)

    for other in seconds:
        forward_second(other)

    waited = qrecv.at[pl.ds(0, narrow - 1)]
    pltpu.make_async_copy(waited, waited, q_recv.at[1]).wait()
    query[...] = jnp.dot(
        picked, qrecv[...].reshape(devices * block, size), preferred_element_type=jnp.float32
    ).astype(jnp.bfloat16)
    maxima[...] = jnp.full(maxima.shape, LOWEST, jnp.float32)
    sums[...] = jnp.zeros(sums.shape, jnp.float32)
    factor = size ** (-0.5) * LOG2E

    def attend(group):
        keys = kv[group, :, :, pl.ds(0, size)].reshape(wide * rows, size)
        values = kv[group, :, :, pl.ds(size, size)].reshape(wide * rows, size)
        cells = jnp.concatenate(
            [cells_ref[pl.ds(u * narrow + group, 1), :] for u in range(wide)], axis=1
        )
        seen = (cells >= start) & (cells <= my_pos)
        wider = jnp.concatenate([values, jnp.ones_like(values)], axis=1)
        scores = lax.dot_general(
            query[...], keys, (((1,), (1,)), ((), ())), preferred_element_type=jnp.float32
        )
        expos, shrinks = [], []
        for h in range(heads):
            part = pl.ds(h * rows, rows)
            shown = jnp.where(seen, scores[h * rows:(h + 1) * rows] * factor, HIDDEN)
            old = maxima[part, :]
            top = jnp.maximum(old, jnp.max(shown, axis=1, keepdims=True))
            expos.append(jnp.exp2(shown - top).astype(jnp.bfloat16))
            shrinks.append(jnp.exp2(old - top))
            maxima[part, :] = top
        product = jnp.dot(
            jnp.concatenate(expos, axis=0), wider, preferred_element_type=jnp.float32
        )
        for h in range(heads):
            part = pl.ds(h * rows, rows)
            sums[part, :] = sums[part, :] * shrinks[h] + product[h * rows:(h + 1) * rows]

    attend(p)
    for other in seconds:
        forward_second(firsts(other, core))
    attend(first)
    take(sibling)
    attend(sibling)
    sibling_first = firsts(sibling, 1 - core)
    take(sibling_first)
    attend(sibling_first)
    sibling_seconds = second_list(sibling, 1 - core)
    for other in seconds:
        attend(other)
    for other in sibling_seconds:
        take(other)
        attend(other)
    for other in seconds:
        attend(firsts(other, core))
    for other in sibling_seconds:
        far = firsts(other, 1 - core)
        take(far)
        attend(far)

    for h in range(heads):
        part = pl.ds(h * rows, rows)
        out_ref[:, h * size:(h + 1) * size] = (
            sums[part, pl.ds(0, size)] / sums[part, pl.ds(size, size)]
        ).astype(jnp.bfloat16)

    spans = (kv.at[0, pl.ds(0, wide - 1)], kv.at[0], kv.at[pl.ds(0, 2 * (outer - 1))], kv.at[pl.ds(0, narrow // 2)])
    for kind, span in enumerate(spans):
        pltpu.make_async_copy(span, span, kv_send.at[kind]).wait()
    for kind, span in enumerate((qsend.at[pl.ds(0, wide - 1)], qrecv.at[pl.ds(0, narrow - 1)])):
        pltpu.make_async_copy(span, span, q_send.at[kind]).wait()


def solution(mesh):
    wide, narrow = mesh.shape["wide"], mesh.shape["narrow"]
    devices = wide * narrow

    def shards(tokens, row_cells, documents, query_weight, key_weight, value_weight):
        rows, width = tokens.shape
        size = key_weight.shape[1]
        heads = query_weight.shape[1] // size
        pair = rows // devices
        block = -(-pair * heads // 16) * 16
        depth = width // CHUNKS
        dims = (wide, narrow, rows, heads, size, block)
        vmem = pl.BlockSpec(memory_space=pltpu.VMEM)
        hbm = pl.BlockSpec(memory_space=pl.ANY)
        flops = 2 * rows * width * (heads + 2) * size + 4 * rows * heads * devices * rows * size
        return pl.pallas_call(
            functools.partial(kernel, dims),
            out_shape=jax.ShapeDtypeStruct((rows, heads * size), jnp.bfloat16),
            in_specs=[hbm, vmem, vmem, hbm, hbm, hbm],
            out_specs=vmem,
            scratch_shapes=[
                pltpu.VMEM((CHUNKS, rows, depth), jnp.bfloat16),
                pltpu.VMEM((CHUNKS, depth, 2 * size), jnp.bfloat16),
                pltpu.VMEM((CHUNKS, depth, heads * size), jnp.bfloat16),
                pltpu.VMEM((narrow, wide, rows, 2 * size), jnp.bfloat16),
                pltpu.VMEM((wide, narrow, block, size), jnp.bfloat16),
                pltpu.VMEM((wide, narrow, block, size), jnp.bfloat16),
                pltpu.VMEM((narrow, wide, block, size), jnp.bfloat16),
                pltpu.VMEM((heads * rows, size), jnp.bfloat16),
                pltpu.VMEM((heads * rows, 1), jnp.float32),
                pltpu.VMEM((heads * rows, 2 * size), jnp.float32),
                pltpu.SemaphoreType.DMA((4, CHUNKS)),
                pltpu.SemaphoreType.DMA((narrow, wide)),
                pltpu.SemaphoreType.DMA((4,)),
                pltpu.SemaphoreType.DMA((2,)),
                pltpu.SemaphoreType.DMA((2,)),
            ],
            compiler_params=pltpu.CompilerParams(
                collective_id=0, has_side_effects=True, vmem_limit_bytes=56 * 1024 * 1024
            ),
            cost_estimate=pl.CostEstimate(
                flops=flops, bytes_accessed=16 * 1024 * 1024, transcendentals=rows * heads * devices * rows
            ),
        )(
            tokens,
            row_cells.reshape(devices, rows),
            documents.reshape(devices, rows),
            query_weight,
            key_weight,
            value_weight,
        )

    in_specs = (P(("wide", "narrow"), None), P(), P(), P(), P(), P())
    return jax.shard_map(
        shards, mesh=mesh, in_specs=in_specs, out_specs=P(("wide", "narrow"), None), check_vma=False
    )
```
